512 devices in a mesh: dp: 512 (over z, y, x, core).
Axes of the slice: x: 4, y: 8, z: 8, core: 2. Of those that a mesh axis runs over, the one named last changes fastest.
Arguments:
- images: float32 [131072, 1152], P('dp'), may hold values from -0.2 to 0.2
- texts: float32 [131072, 1152], P('dp'), may hold values from -0.2 to 0.2
- log_scale: float32 [1], replicated, may hold values from 2 to 2.8
- bias: float32 [1], replicated, may hold values from -3 to -1
Outputs:
- image_grad: float32 [131072, 1152], P('dp')
- text_grad: float32 [131072, 1152], P('dp')
The draws below stay inside these ranges and needn't reach their ends.
All inputs are finite; a program needn't handle non-finite values.
Results may differ from the reference program's by a relative error of at most 0.00012.
Values sent between devices are 32-bit elements; how exact they have to be, the bound alone decides.
A program may use at most 64 MiB of HBM per device.

```python
import jax
import jax.numpy as jnp
from jax import lax

D = 1152
TOK_DEV = 256
STEPS = 4
PAIRS = 131072
N_DP = 512


def levels(rng, dims, cuts, least, high):
    def one(axis_at, blocks):
        draws = jax.random.uniform(jax.random.fold_in(jax.random.fold_in(rng, 6), axis_at), (blocks,), jnp.float32, least / len(cuts), high / len(cuts))
        return jnp.repeat(jnp.exp(draws), dims[axis_at] // blocks).reshape((-1,) + (1,) * (len(dims) - axis_at - 1))

    gain = one(*cuts[0])
    for cut in cuts[1:]:
        gain = gain * one(*cut)
    return gain


def bell_draw(key, shape, deviation, limit, cuts=(), held_as=jnp.bfloat16):
    factor_of = levels(key, shape, cuts, -0.22, 0.18) if cuts else 1.0
    entries = jax.random.normal(key, shape, jnp.float32) * deviation * factor_of
    return jnp.minimum(jnp.maximum(entries, -limit), limit).astype(held_as)


def setup_inputs(seed: int = 0) -> dict:
    streams_of = jax.random.split(jax.random.key(seed), 5)
    images = bell_draw(streams_of[0], (PAIRS, D), 0.03, 0.2, ((0, 512),), jnp.float32)
    texts = bell_draw(streams_of[1], (PAIRS, D), 0.03, 0.2, ((0, 512),), jnp.float32)
    log_scale = jnp.clip(jax.random.uniform(streams_of[2], (1,), jnp.float32, 2.0, 2.8), 2.0, 2.8)
    bias = jnp.clip(jax.random.uniform(streams_of[3], (1,), jnp.float32, -3.0, -1.0), -3.0, -1.0)
    return dict(images=images, texts=texts, log_scale=log_scale, bias=bias)


def reference(images, texts, log_scale, bias):
    scale = jnp.exp(log_scale[0])
    blocks_x = images.reshape(N_DP, TOK_DEV, D)
    blocks_y = texts.reshape(N_DP, TOK_DEV, D)
    diag = jnp.arange(TOK_DEV)[:, None] == jnp.arange(TOK_DEV)[None, :]
    image_grad = jnp.zeros_like(blocks_x)
    text_grad = jnp.zeros_like(blocks_y)
    for step in range(STEPS):
        visit = jnp.roll(blocks_y, step, axis=0)
        logits = scale * jnp.einsum("nbd,ncd->nbc", blocks_x, visit, precision=lax.Precision.HIGHEST) + bias[0]
        if step == 0:
            sign = jnp.where(diag, 1.0, -1.0).astype(jnp.float32)
        else:
            sign = -jnp.ones((TOK_DEV, TOK_DEV), jnp.float32)
        grads = -sign * jax.nn.sigmoid(-sign * logits) * scale
        image_grad = image_grad + jnp.einsum("nbc,ncd->nbd", grads, visit, precision=lax.Precision.HIGHEST)
        contrib = jnp.einsum("nbc,nbd->ncd", grads, blocks_x, precision=lax.Precision.HIGHEST)
        text_grad = text_grad + jnp.roll(contrib, -step, axis=0)
    return image_grad.reshape(N_DP * TOK_DEV, D), text_grad.reshape(N_DP * TOK_DEV, D)
```

```python
import functools

import jax
import jax.numpy as jnp
from jax import lax
from jax.experimental import pallas as pl
from jax.experimental.pallas import tpu as pltpu
from jax.sharding import PartitionSpec as P

MESH = pl.DeviceIdType.MESH
CHUNKS = 4
SIB, D1, D2, D3, E2, E3 = range(6)
NT = (((1,), (1,)), ((), ()))


def halves(value):
    high = value.astype(jnp.bfloat16)
    return high, (value - high.astype(jnp.float32)).astype(jnp.bfloat16)


def product(a, b, dims=(((1,), (0,)), ((), ()))):
    (ah, al), (bh, bl) = a, b

    def dot(u, v):
        return lax.dot_general(u, v, dims, preferred_element_type=jnp.float32)

    return dot(ah, bh) + (dot(ah, bl) + dot(al, bh))


def kernel(n, x_ref, y_ref, ls_ref, bias_ref, xg_ref, yg_ref, own, high, low, held, acc, scale, load_sem, out_sem, send_sem, recv_sem, left_sem):
    me = lax.axis_index("dp")
    core = lax.rem(me, 2)
    sib = me + 1 - 2 * core
    right, left = lax.rem(me + 2, n), lax.rem(me + n - 2, n)
    front, back = lax.rem(me + n - 2 + 4 * core, n), lax.rem(me + n + 2 - 4 * core, n)
    rows = own.shape[1]
    part = rows // CHUNKS

    barrier = pltpu.get_barrier_semaphore()
    for peer in (left, sib):
        pl.semaphore_signal(barrier, inc=1, device_id=(peer,), device_id_type=MESH)

    def load(slot, ref):
        return pltpu.make_async_copy(ref, own.at[slot], load_sem.at[slot])

    @pl.when(core == 0)
    def _():
        load(0, x_ref).start()
        load(1, y_ref).start()

    @pl.when(core == 1)
    def _():
        load(0, y_ref).start()
        load(1, x_ref).start()

    def send(src, slot, chunk, peer):
        at = pl.ds(chunk * part, part)
        return pltpu.make_async_remote_copy(
            src_ref=src.at[at],
            dst_ref=held.at[slot, at],
            send_sem=send_sem.at[slot, chunk],
            recv_sem=recv_sem.at[slot, chunk],
            device_id=(peer,),
            device_id_type=MESH,
        )

    def send_a(chunk):
        return send(own.at[0], E2, chunk, front)

    def send_b(chunk):
        return send(own.at[1], D2, chunk, back)

    def send_sib(chunk):
        return send(own.at[1], SIB, chunk, sib)

    def pass_e2(chunk):
        return send(held.at[E2], D1, chunk, sib)

    def pass_d2(chunk):
        return send(held.at[D2], E3, chunk, sib)

    def relay_d1(chunk):
        return send(held.at[D1], D3, chunk, back)

    def start(which):
        for chunk in range(CHUNKS):
            which(chunk).start()

    load(0, x_ref).wait()
    load(1, y_ref).wait()
    pl.semaphore_wait(barrier, 2)
    pl.semaphore_signal(left_sem, inc=1, device_id=(right,), device_id_type=MESH)

    @pl.when(core == 0)
    def _():
        start(send_b)
        pl.semaphore_wait(left_sem, 1)
        start(send_a)

    @pl.when(core == 1)
    def _():
        start(send_a)
        pl.semaphore_wait(left_sem, 1)
        start(send_b)

    start(send_sib)

    scale[...] = jnp.exp(jnp.full(scale.shape, ls_ref[0], jnp.float32))
    offset = bias_ref[0]
    for slot in range(2):
        high[slot], low[slot] = halves(own[slot])

    def add_pairs(mine, other, count, first=False):
        theirs = halves(other)
        times = scale[:, :count]
        logits = product((high[mine], low[mine]), theirs, NT) * times + offset
        if first:
            shape = (rows, count)
            diag = lax.broadcasted_iota(jnp.int32, shape, 0) == lax.broadcasted_iota(jnp.int32, shape, 1)
            grads = jnp.where(diag, -times, times) / (1.0 + jnp.exp(jnp.where(diag, logits, -logits)))
        else:
            grads = times / (1.0 + jnp.exp(-logits))
        term = product(halves(grads), theirs)
        if first:
            acc[mine] = term
        else:
            acc[mine] += term

    add_pairs(0, own[1], rows, True)
    add_pairs(1, own[0], rows, True)
    for chunk in range(CHUNKS):
        send_sib(chunk).wait_recv()
    add_pairs(1, held[SIB], rows)

    half = CHUNKS // 2
    for chunk in range(CHUNKS):
        pass_slots = ((send_a, pass_e2), (send_b, pass_d2), (pass_e2, relay_d1))
        for arrives, leaves in pass_slots:
            arrives(chunk).wait_recv()
            leaves(chunk).start()
        if chunk % half == half - 1:
            for c in range(chunk + 1 - half, chunk + 1):
                pass_d2(c).wait_recv()
            at = pl.ds((chunk + 1 - half) * part, half * part)
            for mine, slot in ((1, E2), (1, E3), (0, D1), (0, D2)):
                add_pairs(mine, held[slot, at], half * part)

    def store(slot, ref):
        return pltpu.make_async_copy(acc.at[slot], ref, out_sem.at[slot])

    @pl.when(core == 0)
    def _():
        store(1, yg_ref).start()

    @pl.when(core == 1)
    def _():
        store(1, xg_ref).start()

    for chunk in range(CHUNKS):
        relay_d1(chunk).wait_recv()
        add_pairs(0, held[D3, pl.ds(chunk * part, part)], part)

    @pl.when(core == 0)
    def _():
        store(0, xg_ref).start()

    @pl.when(core == 1)
    def _():
        store(0, yg_ref).start()

    for which in (send_a, send_b, send_sib, pass_e2, pass_d2, relay_d1):
        for chunk in range(CHUNKS):
            which(chunk).wait_send()
    store(0, xg_ref).wait()
    store(1, yg_ref).wait()


def per_device(n, images, texts, log_scale, bias):
    rows, width = images.shape
    block = (rows, width)
    return pl.pallas_call(
        functools.partial(kernel, n),
        out_shape=(jax.ShapeDtypeStruct(block, jnp.float32),) * 2,
        in_specs=[pl.BlockSpec(memory_space=pl.ANY)] * 2 + [pl.BlockSpec(memory_space=pltpu.SMEM)] * 2,
        out_specs=(pl.BlockSpec(memory_space=pl.ANY),) * 2,
        scratch_shapes=[
            pltpu.VMEM((2, *block), jnp.float32),
            pltpu.VMEM((2, *block), jnp.bfloat16),
            pltpu.VMEM((2, *block), jnp.bfloat16),
            pltpu.VMEM((6, *block), jnp.float32),
            pltpu.VMEM((2, *block), jnp.float32),
            pltpu.VMEM((1, rows), jnp.float32),
            pltpu.SemaphoreType.DMA((2,)),
            pltpu.SemaphoreType.DMA((2,)),
            pltpu.SemaphoreType.DMA((6, CHUNKS)),
            pltpu.SemaphoreType.DMA((6, CHUNKS)),
            pltpu.SemaphoreType.REGULAR,
        ],
        compiler_params=pltpu.CompilerParams(collective_id=0, has_side_effects=True, vmem_limit_bytes=56 * 2**20),
    )(images, texts, log_scale, bias)


def solution(mesh):
    return jax.shard_map(
        functools.partial(per_device, mesh.shape["dp"]),
        mesh=mesh,
        in_specs=(P("dp", None), P("dp", None), P(), P()),
        out_specs=(P("dp", None), P("dp", None)),
        check_vma=False,
    )
```

```python
import functools

import jax
import jax.numpy as jnp
from jax import lax
from jax.experimental import pallas as pl
from jax.experimental.pallas import tpu as pltpu
from jax.sharding import PartitionSpec as P

MESH = pl.DeviceIdType.MESH
CHUNKS = 4
SIB, D1, D2, D3, E2, E3 = range(6)
HALVES = ((0, range(0, 2)), (2, range(2, 4)))
TAIL = (range(0, 2), range(2, 3), range(3, 4))
NT = (((1,), (1,)), ((), ()))


def halves(value):
    high = value.astype(jnp.bfloat16)
    return high, (value - high.astype(jnp.float32)).astype(jnp.bfloat16)


def dot(a, b, dims=(((1,), (0,)), ((), ()))):
    return lax.dot_general(a, b, dims, preferred_element_type=jnp.float32)


def kernel(n, x_ref, y_ref, ls_ref, bias_ref, a_acc, b_acc, own, high, low, held, stack, scale, load_sem, send_sem, recv_sem, left_sem):
    me = lax.axis_index("dp")
    core, chip = lax.rem(me, 2), lax.div(me, 2)
    sib = me + 1 - 2 * core
    right, left = lax.rem(me + 2, n), lax.rem(me + n - 2, n)
    front, back = lax.rem(me + n - 2 + 4 * core, n), lax.rem(me + n + 2 - 4 * core, n)
    rows = own.shape[1]
    part, half = rows // CHUNKS, rows // 2
    first, last = chip == 0, chip == n // 2 - 1

    barrier = pltpu.get_barrier_semaphore()

    def greet(peer):
        pl.semaphore_signal(barrier, inc=1, device_id=(peer,), device_id_type=MESH)

    greet(sib)
    greet(left)
    pl.when(jnp.logical_not(last))(lambda: greet(right))

    def load(slot, ref):
        return pltpu.make_async_copy(ref, own.at[slot], load_sem.at[slot])

    @pl.when(core == 0)
    def _():
        load(0, x_ref).start()
        load(1, y_ref).start()

    @pl.when(core == 1)
    def _():
        load(0, y_ref).start()
        load(1, x_ref).start()

    def send(src, slot, chunk, peer):
        at = pl.ds(chunk * part, part)
        return pltpu.make_async_remote_copy(
            src_ref=src.at[at],
            dst_ref=held.at[slot, at],
            send_sem=send_sem.at[slot, chunk],
            recv_sem=recv_sem.at[slot, chunk],
            device_id=(peer,),
            device_id_type=MESH,
        )

    def send_a(chunk):
        return send(own.at[0], E2, chunk, front)

    def send_b(chunk):
        return send(own.at[1], D2, chunk, back)

    def send_sib(chunk):
        return send(own.at[1], SIB, chunk, sib)

    def pass_e2(chunk):
        return send(held.at[E2], D1, chunk, sib)

    def pass_d2(chunk):
        return send(held.at[D2], E3, chunk, sib)

    def relay_d1(chunk):
        return send(held.at[D1], D3, chunk, back)

    def start(which):
        for chunk in range(CHUNKS):
            which(chunk).start()

    def arrive(which, chunks=range(CHUNKS)):
        for chunk in chunks:
            which(chunk).wait_recv()

    load(0, x_ref).wait()
    load(1, y_ref).wait()
    pl.semaphore_wait(barrier, jnp.where(first, 2, 3))
    pl.when(last)(lambda: pl.semaphore_signal(left_sem, inc=1, device_id=(right,), device_id_type=MESH))

    def start_right():
        pl.when(core == 0)(lambda: start(send_b))
        pl.when(core == 1)(lambda: start(send_a))

    def start_left():
        pl.when(core == 0)(lambda: start(send_a))
        pl.when(core == 1)(lambda: start(send_b))

    start_right()
    pl.when(jnp.logical_not(first))(start_left)
    start(send_sib)

    scale[...] = jnp.exp(jnp.full(scale.shape, ls_ref[0], jnp.float32))
    offset = bias_ref[0]
    for slot in range(2):
        high[slot], low[slot] = halves(own[slot])

    def add_pairs(mine, block, at, count, same=False):
        acc = (a_acc, b_acc)[mine]
        oh, ol = halves(block[pl.ds(at, count)])
        stack[:count], stack[count : 2 * count], stack[2 * count : 3 * count] = oh, ol, oh
        times = scale[:, :count]
        wide = dot(high[mine], stack[: 2 * count], NT)
        logits = (wide[:, :count] + (wide[:, count:] + dot(low[mine], oh, NT))) * times + offset
        if same:
            shape = (rows, count)
            diag = lax.broadcasted_iota(jnp.int32, shape, 0) == lax.broadcasted_iota(jnp.int32, shape, 1) + at
            grads = jnp.where(diag, -times, times) / (1.0 + jnp.exp(jnp.where(diag, logits, -logits)))
        else:
            grads = times / (1.0 + jnp.exp(-logits))
        gh, gl = halves(grads)
        term = dot(jnp.concatenate([gh, gh, gl], axis=1), stack[: 3 * count])
        if same and at == 0:
            acc[...] = term
        else:
            acc[...] += term

    for at in (0, half):
        add_pairs(0, own.at[1], at, half, True)
        add_pairs(1, own.at[0], at, half, True)
    for at, chunks in HALVES:
        arrive(send_sib, chunks)
        add_pairs(1, held.at[SIB], at * part, half)

    def add_e(at, chunks):
        add_pairs(1, held.at[E2], at * part, half)
        arrive(pass_d2, chunks)
        add_pairs(1, held.at[E3], at * part, half)

    def add_d(at):
        add_pairs(0, held.at[D1], at * part, half)
        add_pairs(0, held.at[D2], at * part, half)

    def take_e(chunk):
        send_a(chunk).wait_recv()
        pass_e2(chunk).start()

    def take_d(chunk):
        send_b(chunk).wait_recv()
        pass_d2(chunk).start()

    def take_d1(chunk):
        pass_e2(chunk).wait_recv()
        relay_d1(chunk).start()

    def add_d3(chunks):
        arrive(relay_d1, chunks)
        add_pairs(0, held.at[D3], chunks[0] * part, len(chunks) * part)

    @pl.when(jnp.logical_not(first))
    def _():
        for at, chunks in HALVES:
            for chunk in chunks:
                take_e(chunk)
                take_d(chunk)
                take_d1(chunk)
            add_e(at, chunks)
            add_d(at)
        for chunks in TAIL:
            add_d3(chunks)

    @pl.when(first)
    def _():
        pl.semaphore_wait(left_sem, 1)
        start_left()

    @pl.when(jnp.logical_and(first, core == 0))
    def _():
        for at, chunks in HALVES:
            for chunk in chunks:
                take_e(chunk)
            add_e(at, chunks)
        for at, chunks in HALVES:
            for chunk in chunks:
                take_d(chunk)
                take_d1(chunk)
            add_d(at)
        for chunks in TAIL:
            add_d3(chunks)

    @pl.when(jnp.logical_and(first, core == 1))
    def _():
        for at, chunks in HALVES:
            for chunk in chunks:
                take_d(chunk)
                take_d1(chunk)
            add_d(at)
        for (at, chunks), tail in zip(HALVES, TAIL):
            for chunk in chunks:
                take_e(chunk)
            add_d3(tail)
            add_e(at, chunks)
        for chunks in TAIL[2:]:
            add_d3(chunks)

    for which in (send_a, send_b, send_sib, pass_e2, pass_d2, relay_d1):
        for chunk in range(CHUNKS):
            which(chunk).wait_send()


def place(a_ref, b_ref, xg_ref, yg_ref, sem):
    core = lax.rem(lax.axis_index("dp"), 2)

    def put(slot, ref):
        return pltpu.make_async_copy((a_ref, b_ref)[slot], ref, sem.at[slot])

    @pl.when(core == 0)
    def _():
        put(0, xg_ref).start()
        put(1, yg_ref).start()

    @pl.when(core == 1)
    def _():
        put(0, yg_ref).start()
        put(1, xg_ref).start()

    put(0, xg_ref).wait()
    put(1, yg_ref).wait()


def per_device(n, images, texts, log_scale, bias):
    rows, width = images.shape
    block = (rows, width)
    hbm = [pltpu.with_memory_space_constraint(z, pltpu.HBM) for z in (images, texts)]
    grads = pl.pallas_call(
        functools.partial(kernel, n),
        out_shape=(pltpu.VMEM(block, jnp.float32),) * 2,
        in_specs=[pl.BlockSpec(memory_space=pl.ANY)] * 2 + [pl.BlockSpec(memory_space=pltpu.SMEM)] * 2,
        out_specs=(pl.BlockSpec(memory_space=pltpu.VMEM),) * 2,
        scratch_shapes=[
            pltpu.VMEM((2, *block), jnp.float32),
            pltpu.VMEM((2, *block), jnp.bfloat16),
            pltpu.VMEM((2, *block), jnp.bfloat16),
            pltpu.VMEM((6, *block), jnp.float32),
            pltpu.VMEM((3 * rows // 2, width), jnp.bfloat16),
            pltpu.VMEM((1, rows), jnp.float32),
            pltpu.SemaphoreType.DMA((2,)),
            pltpu.SemaphoreType.DMA((6, CHUNKS)),
            pltpu.SemaphoreType.DMA((6, CHUNKS)),
            pltpu.SemaphoreType.REGULAR,
        ],
        compiler_params=pltpu.CompilerParams(collective_id=0, has_side_effects=True, vmem_limit_bytes=40 * 2**20),
    )(*hbm, log_scale, bias)
    return pl.pallas_call(
        place,
        out_shape=(pltpu.HBM(block, jnp.float32),) * 2,
        in_specs=[pl.BlockSpec(memory_space=pl.ANY)] * 2,
        out_specs=(pl.BlockSpec(memory_space=pl.ANY),) * 2,
        scratch_shapes=[pltpu.SemaphoreType.DMA((2,))],
    )(*(pltpu.with_memory_space_constraint(z, pltpu.VMEM) for z in grads))


def solution(mesh):
    return jax.shard_map(
        functools.partial(per_device, mesh.shape["dp"]),
        mesh=mesh,
        in_specs=(P("dp", None), P("dp", None), P(), P()),
        out_specs=(P("dp", None), P("dp", None)),
        check_vma=False,
    )
```

```python
import functools

import jax
import jax.numpy as jnp
from jax import lax
from jax.experimental import pallas as pl
from jax.experimental.pallas import tpu as pltpu
from jax.sharding import PartitionSpec as P

MESH = pl.DeviceIdType.MESH
A, B, SIB, D1, D2, D3, E2, E3 = range(8)
NT = (((1,), (1,)), ((), ()))
START = ((B, 0), (B, 1), (A, 0), (A, 1), (SIB, 0), (SIB, 1))
LOCAL = len(START)
USUAL = START + ((E2, 0), (D1, 0), (E2, 1), (D1, 1), (D2, 0), (E3, 0), (D2, 1), (E3, 1), (D3, 0), (D3, 1))
FIRST = (
    START + ((E2, 0), (D1, 0), (E2, 1), (D1, 1), (E3, 0), (E3, 1), (D2, 0), (D2, 1), (D3, 0), (D3, 1)),
    START + ((D1, 0), (E2, 0), (D1, 1), (E2, 1), (D2, 0), (D2, 1), (E3, 0), (D3, 0), (E3, 1), (D3, 1)),
)
LAST = (
    START + ((D1, 0), (D1, 1), (D2, 0), (E2, 0), (D2, 1), (E2, 1), (D3, 0), (E3, 0), (D3, 1), (E3, 1)),
    START + ((E2, 0), (E2, 1), (E3, 0), (D1, 0), (E3, 1), (D1, 1), (D2, 0), (D2, 1), (D3, 0), (D3, 1)),
)


def halves(value):
    high = value.astype(jnp.bfloat16)
    return high, (value - high.astype(jnp.float32)).astype(jnp.bfloat16)


def dot(a, b, dims=(((1,), (0,)), ((), ()))):
    return lax.dot_general(a, b, dims, preferred_element_type=jnp.float32)


def pick(index, values):
    result = values[0]
    for k in range(1, len(values)):
        if values[k] != values[k - 1]:
            result = jnp.where(index >= k, values[k], result)
    return result


def kernel(n, x_ref, y_ref, ls_ref, bias_ref, acc, pool, high, low, stack, scale, load_sem, send_sem, recv_sem, left_sem):
    me = lax.axis_index("dp")
    core, chip = lax.rem(me, 2), lax.div(me, 2)
    sib = me + 1 - 2 * core
    right, left = lax.rem(me + 2, n), lax.rem(me + n - 2, n)
    front, back = lax.rem(me + n - 2 + 4 * core, n), lax.rem(me + n + 2 - 4 * core, n)
    rows = pool.shape[1]
    half = rows // 2
    first, last = chip == 0, chip == n // 2 - 1

    barrier = pltpu.get_barrier_semaphore()

    def greet(peer):
        pl.semaphore_signal(barrier, inc=1, device_id=(peer,), device_id_type=MESH)

    greet(sib)
    greet(left)
    pl.when(jnp.logical_not(last))(lambda: greet(right))
    opens, early, closes = first & (core == 0), first & (core == 1), last & (core == 1)
    before, after = lax.rem(me + n - 1, n), lax.rem(me + 1, n)
    pl.when(opens)(lambda: greet(before))

    def load(slot, ref):
        return pltpu.make_async_copy(ref, pool.at[slot], load_sem.at[slot])

    @pl.when(core == 0)
    def _():
        load(A, x_ref).start()
        load(B, y_ref).start()

    @pl.when(core == 1)
    def _():
        load(A, y_ref).start()
        load(B, x_ref).start()

    def send(src, dst, h, peer, sem=None):
        at = pl.ds(h * half, half)
        return pltpu.make_async_remote_copy(
            src_ref=pool.at[src, at],
            dst_ref=pool.at[dst, at],
            send_sem=send_sem.at[dst if sem is None else sem, h],
            recv_sem=recv_sem.at[dst, h],
            device_id=(peer,),
            device_id_type=MESH,
        )

    def send_a(h):
        return send(A, E2, h, front)

    def send_b(h):
        return send(B, D2, h, back)

    def send_sib(h):
        return send(B, SIB, h, sib)

    def pass_e2(h):
        return send(E2, D1, h, sib)

    def pass_d2(h):
        return send(D2, E3, h, sib)

    def relay_d1(h):
        return send(D1, D3, h, back)

    def relay_e2(h):
        return send(E2, D3, h, before, A)

    def start(which):
        which(0).start()
        which(1).start()

    acc[...] = jnp.zeros_like(acc)
    scale[...] = jnp.exp(jnp.full(scale.shape, ls_ref[0], jnp.float32))
    offset = bias_ref[0]
    load(A, x_ref).wait()
    load(B, y_ref).wait()
    pl.semaphore_wait(barrier, jnp.where(first, 2, jnp.where(closes, 4, 3)))
    pl.when(last)(lambda: pl.semaphore_signal(left_sem, inc=1, device_id=(right,), device_id_type=MESH))
    pl.when(closes)(lambda: pl.semaphore_signal(left_sem, inc=1, device_id=(after,), device_id_type=MESH))
    pl.when(opens)(lambda: start(send_b))
    pl.when(jnp.logical_not(opens))(lambda: start(send_a))
    start(send_sib)
    for slot in range(2):
        high[slot], low[slot] = halves(pool[slot])

    def take_e2(h):
        send_a(h).wait_recv()
        pass_e2(h).start()
        pl.when(opens)(lambda: relay_e2(h).start())

    def take_d2(h):
        send_b(h).wait_recv()
        pass_d2(h).start()

    def take_d1(h):
        pass_e2(h).wait_recv()
        pl.when(jnp.logical_not(early))(lambda: relay_d1(h).start())

    def open_left():
        pl.when(early)(lambda: pl.semaphore_wait(left_sem, 1))
        pl.when(opens)(lambda: pl.semaphore_wait(left_sem, 2))
        pl.when(opens)(lambda: start(send_a))

    def start_later():
        pl.when(jnp.logical_not(opens))(lambda: start(send_b))

    def add_pairs(mine, slot, h):
        at = pl.multiple_of(h * half, half)
        oh, ol = halves(pool[slot, pl.ds(at, half)])
        stack[:half], stack[half : 2 * half], stack[2 * half :] = oh, ol, oh
        times = scale[...]
        wide = dot(high[mine], stack[: 2 * half], NT)
        logits = (wide[:, :half] + (wide[:, half:] + dot(low[mine], oh, NT))) * times + offset
        shape = (rows, half)
        gap = lax.broadcasted_iota(jnp.int32, shape, 0) - lax.broadcasted_iota(jnp.int32, shape, 1)
        positive = gap == jnp.where(slot <= B, at, rows)
        grads = jnp.where(positive, -times, times) / (1.0 + jnp.exp(jnp.where(positive, logits, -logits)))
        gh, gl = halves(grads)
        acc[mine] += dot(jnp.concatenate([gh, gh, gl], axis=1), stack[...])

    def by_place(usual, zero, one, last_zero, last_one):
        ends = jnp.where(first, jnp.where(core == 0, zero, one), jnp.where(core == 0, last_zero, last_one))
        return jnp.where(first | last, ends, usual)

    def step_of(block, h):
        return by_place(*(tasks.index((block, h)) for tasks in (USUAL, *FIRST, *LAST)))

    def recv(which, h):
        return lambda: which(h).wait_recv()

    events = [(jnp.int32(LOCAL), open_left), (jnp.where(first, LOCAL + 2, LOCAL), start_later)]
    for h in range(2):
        events += [
            (step_of(SIB, h), recv(send_sib, h)),
            (step_of(E2, h), functools.partial(take_e2, h)),
            (step_of(D2, h), functools.partial(take_d2, h)),
            (step_of(E3, h), recv(pass_d2, h)),
            (step_of(D1, h), functools.partial(take_d1, h)),
            (step_of(D3, h), recv(relay_d1, h)),
        ]

    def by_order(i, part):
        return [pick(i, [task[part] for task in tasks]) for tasks in (USUAL, *FIRST, *LAST)]

    def step(i, _):
        for at_step, event in events:
            pl.when(i == at_step)(event)
        slot, h = (by_place(*by_order(i, part)) for part in range(2))
        mine = jnp.where((slot == A) | (slot == SIB) | (slot >= E2), 1, 0)
        add_pairs(mine, slot, h)
        return 0

    lax.fori_loop(0, len(USUAL), step, 0)

    for h in range(2):
        for which in (send_a, send_b, send_sib, pass_e2, pass_d2):
            which(h).wait_send()
        pl.when(jnp.logical_not(early))(lambda: relay_d1(h).wait_send())
        pl.when(opens)(lambda: relay_e2(h).wait_send())


def place(acc, xg_ref, yg_ref, sem):
    core = lax.rem(lax.axis_index("dp"), 2)

    def put(slot, ref):
        return pltpu.make_async_copy(acc.at[slot], ref, sem.at[slot])

    @pl.when(core == 0)
    def _():
        put(0, xg_ref).start()
        put(1, yg_ref).start()

    @pl.when(core == 1)
    def _():
        put(0, yg_ref).start()
        put(1, xg_ref).start()

    put(0, xg_ref).wait()
    put(1, yg_ref).wait()


def per_device(n, images, texts, log_scale, bias):
    rows, width = images.shape
    block = (rows, width)
    hbm = [pltpu.with_memory_space_constraint(z, pltpu.HBM) for z in (images, texts)]
    grads = pl.pallas_call(
        functools.partial(kernel, n),
        out_shape=pltpu.VMEM((2, *block), jnp.float32),
        in_specs=[pl.BlockSpec(memory_space=pl.ANY)] * 2 + [pl.BlockSpec(memory_space=pltpu.SMEM)] * 2,
        out_specs=pl.BlockSpec(memory_space=pltpu.VMEM),
        scratch_shapes=[
            pltpu.VMEM((8, *block), jnp.float32),
            pltpu.VMEM((2, *block), jnp.bfloat16),
            pltpu.VMEM((2, *block), jnp.bfloat16),
            pltpu.VMEM((3 * rows // 2, width), jnp.bfloat16),
            pltpu.VMEM((1, rows // 2), jnp.float32),
            pltpu.SemaphoreType.DMA((2,)),
            pltpu.SemaphoreType.DMA((8, 2)),
            pltpu.SemaphoreType.DMA((8, 2)),
            pltpu.SemaphoreType.REGULAR,
        ],
        compiler_params=pltpu.CompilerParams(collective_id=0, has_side_effects=True, vmem_limit_bytes=40 * 2**20),
    )(*hbm, log_scale, bias)
    return pl.pallas_call(
        place,
        out_shape=(pltpu.HBM(block, jnp.float32),) * 2,
        in_specs=[pl.BlockSpec(memory_space=pl.ANY)],
        out_specs=(pl.BlockSpec(memory_space=pl.ANY),) * 2,
        scratch_shapes=[pltpu.SemaphoreType.DMA((2,))],
    )(pltpu.with_memory_space_constraint(grads, pltpu.VMEM))


def solution(mesh):
    return jax.shard_map(
        functools.partial(per_device, mesh.shape["dp"]),
        mesh=mesh,
        in_specs=(P("dp", None), P("dp", None), P(), P()),
        out_specs=(P("dp", None), P("dp", None)),
        check_vma=False,
    )
```

```python
import functools

import jax
import jax.numpy as jnp
from jax import lax
from jax.experimental import pallas as pl
from jax.experimental.pallas import tpu as pltpu
from jax.sharding import PartitionSpec as P

MESH = pl.DeviceIdType.MESH
A, B, SIB, D1, D2, D3, E2, E3 = range(8)
NT = (((1,), (1,)), ((), ()))
START = ((B, 0), (B, 1), (A, 0), (A, 1), (SIB, 0), (SIB, 1))
LOCAL = len(START)
USUAL = START + ((E2, 0), (D2, 0), (D1, 0), (E3, 0), (E2, 1), (D2, 1), (D1, 1), (E3, 1), (D3, 0), (D3, 1))
FIRST = (
    START + ((E3, 0), (E2, 0), (D1, 0), (E3, 1), (E2, 1), (D1, 1), (D2, 0), (D2, 1), (D3, 0), (D3, 1)),
    START + ((D2, 0), (D1, 0), (E2, 0), (D2, 1), (E2, 1), (D1, 1), (E3, 0), (D3, 0), (E3, 1), (D3, 1)),
)
LAST = (
    USUAL,
    START + ((E2, 0), (D1, 0), (E3, 0), (D2, 0), (E2, 1), (D1, 1), (E3, 1), (D2, 1), (D3, 0), (D3, 1)),
)


def halves(value):
    high = value.astype(jnp.bfloat16)
    return high, (value - high.astype(jnp.float32)).astype(jnp.bfloat16)


def dot(a, b, dims=(((1,), (0,)), ((), ()))):
    return lax.dot_general(a, b, dims, preferred_element_type=jnp.float32)


def pick(index, values):
    result = values[0]
    for k in range(1, len(values)):
        if values[k] != values[k - 1]:
            result = jnp.where(index >= k, values[k], result)
    return result


def kernel(n, x_ref, y_ref, ls_ref, bias_ref, acc, pool, high, low, stack, scale, load_sem, send_sem, recv_sem, left_sem):
    me = lax.axis_index("dp")
    core, chip = lax.rem(me, 2), lax.div(me, 2)
    sib = me + 1 - 2 * core
    right, left = lax.rem(me + 2, n), lax.rem(me + n - 2, n)
    front, back = lax.rem(me + n - 2 + 4 * core, n), lax.rem(me + n + 2 - 4 * core, n)
    rows = pool.shape[1]
    half = rows // 2
    first, last = chip == 0, chip == n // 2 - 1

    barrier = pltpu.get_barrier_semaphore()

    def greet(peer):
        pl.semaphore_signal(barrier, inc=1, device_id=(peer,), device_id_type=MESH)

    cross = lax.rem(me + n - 1 + 2 * core, n)
    opens, early, closes = first & (core == 0), first & (core == 1), last & (core == 1)
    greet(sib)
    greet(left)
    pl.when(jnp.logical_not(last))(lambda: greet(right))
    pl.when(jnp.logical_not(closes))(lambda: greet(cross))

    def load(slot, ref):
        return pltpu.make_async_copy(ref, pool.at[slot], load_sem.at[slot])

    @pl.when(core == 0)
    def _():
        load(A, x_ref).start()
        load(B, y_ref).start()

    @pl.when(core == 1)
    def _():
        load(A, y_ref).start()
        load(B, x_ref).start()

    def transfer(src, dst, sent, received, peer):
        return pltpu.make_async_remote_copy(
            src_ref=src, dst_ref=dst, send_sem=sent, recv_sem=received, device_id=(peer,), device_id_type=MESH
        )

    def copy(src, dst, at, sent, received, peer):
        return transfer(pool.at[src, at], pool.at[dst, at], sent, received, peer)

    def send(src, dst, h, peer):
        return copy(src, dst, pl.ds(h * half, half), send_sem.at[dst, h], recv_sem.at[dst, h], peer)

    def relay(src, h, piece, sent, peer):
        at = pl.ds(h * half + piece * (half // 2), half // 2)
        return copy(src, D3, at, send_sem.at[sent, h], recv_sem.at[(D3, A)[piece], h], peer)

    def send_a(h):
        return send(A, E2, h, front)

    def send_b(h):
        return send(B, D2, h, back)

    def send_sib(h):
        return send(B, SIB, h, sib)

    def pass_e2(h):
        return send(E2, D1, h, sib)

    def pass_d2(h):
        return send(D2, E3, h, sib)

    def relay_d1(h):
        return relay(D1, h, 0, D3, back)

    def relay_e2(h):
        return relay(E2, h, 1, A, cross)

    def stand_in(h):
        return relay(E2, h, 0, B, cross)

    def start(which):
        which(0).start()
        which(1).start()

    pl.semaphore_wait(barrier, jnp.where(opens, 2, jnp.where(early, 3, 4)))
    pl.when(last)(lambda: pl.semaphore_signal(left_sem, inc=1, device_id=(right,), device_id_type=MESH))
    pl.when(closes)(lambda: pl.semaphore_signal(left_sem, inc=1, device_id=(cross,), device_id_type=MESH))
    behind = early | (last & (core == 0))

    def start_from(ref, dst, peer):
        for h in range(2):
            at = pl.ds(h * half, half)
            transfer(ref.at[at], pool.at[dst, at], send_sem.at[dst, h], recv_sem.at[dst, h], peer).start()

    for parity, (a_ref, b_ref) in enumerate(((x_ref, y_ref), (y_ref, x_ref))):
        here = core == parity
        pl.when(here & jnp.logical_not(opens))(functools.partial(start_from, a_ref, E2, front))
        pl.when(here & jnp.logical_not(behind))(functools.partial(start_from, b_ref, D2, back))
        pl.when(here)(functools.partial(start_from, b_ref, SIB, sib))
    acc[...] = jnp.zeros_like(acc)
    scale[...] = jnp.exp(jnp.full(scale.shape, ls_ref[0], jnp.float32))
    offset = bias_ref[0]
    load(A, x_ref).wait()
    load(B, y_ref).wait()
    for slot in range(2):
        high[slot], low[slot] = halves(pool[slot])

    def take_e2(h):
        send_a(h).wait_recv()
        pass_e2(h).start()
        waits = opens | closes
        pl.when(jnp.logical_not(waits))(lambda: relay_e2(h).start())
        if h == 1:
            pl.when(waits)(lambda: start(relay_e2))
            pl.when(opens)(lambda: start(stand_in))

    def take_d2(h):
        send_b(h).wait_recv()
        pass_d2(h).start()

    def take_d1(h):
        pass_e2(h).wait_recv()
        pl.when(jnp.logical_not(early))(lambda: relay_d1(h).start())

    def open_left():
        pl.when(early)(lambda: pl.semaphore_wait(left_sem, 1))
        pl.when(opens)(lambda: pl.semaphore_wait(left_sem, 2))
        pl.when(opens)(lambda: start(send_a))

    def start_later():
        pl.when(behind)(lambda: start(send_b))

    def add_pairs(mine, slot, h):
        at = pl.multiple_of(h * half, half)
        oh, ol = halves(pool[slot, pl.ds(at, half)])
        stack[:half], stack[half : 2 * half], stack[2 * half :] = oh, ol, oh
        times = scale[...]
        wide = dot(high[mine], stack[: 2 * half], NT)
        logits = (wide[:, :half] + (wide[:, half:] + dot(low[mine], oh, NT))) * times + offset
        shape = (rows, half)
        gap = lax.broadcasted_iota(jnp.int32, shape, 0) - lax.broadcasted_iota(jnp.int32, shape, 1)
        positive = gap == jnp.where(slot <= B, at, rows)
        grads = jnp.where(positive, -times, times) / (1.0 + jnp.exp(jnp.where(positive, logits, -logits)))
        gh, gl = halves(grads)
        acc[mine] += dot(jnp.concatenate([gh, gh, gl], axis=1), stack[...])

    def by_place(usual, zero, one, last_zero, last_one):
        ends = jnp.where(first, jnp.where(core == 0, zero, one), jnp.where(core == 0, last_zero, last_one))
        return jnp.where(first | last, ends, usual)

    def step_of(block, h):
        return by_place(*(tasks.index((block, h)) for tasks in (USUAL, *FIRST, *LAST)))

    def recv(which, h):
        return lambda: which(h).wait_recv()

    events = [(jnp.int32(LOCAL), open_left), (jnp.int32(LOCAL), start_later)]
    for h in range(2):
        events += [
            (step_of(SIB, h), recv(send_sib, h)),
            (step_of(E2, h), functools.partial(take_e2, h)),
            (step_of(D2, h), functools.partial(take_d2, h)),
            (step_of(E3, h), recv(pass_d2, h)),
            (step_of(D1, h), functools.partial(take_d1, h)),
            (step_of(D3, h), recv(relay_d1, h)),
            (step_of(D3, h), recv(relay_e2, h)),
        ]

    def by_order(i, part):
        return [pick(i, [task[part] for task in tasks]) for tasks in (USUAL, *FIRST, *LAST)]

    def step(i, _):
        for at_step, event in events:
            pl.when(i == at_step)(event)
        slot, h = (by_place(*by_order(i, part)) for part in range(2))
        mine = jnp.where((slot == A) | (slot == SIB) | (slot >= E2), 1, 0)
        add_pairs(mine, slot, h)
        return 0

    lax.fori_loop(0, len(USUAL), step, 0)

    for h in range(2):
        for which in (send_a, send_b, send_sib, pass_e2, pass_d2):
            which(h).wait_send()
        relay_e2(h).wait_send()
        pl.when(jnp.logical_not(early))(lambda: relay_d1(h).wait_send())
        pl.when(opens)(lambda: stand_in(h).wait_send())


def place(acc, xg_ref, yg_ref, sem):
    core = lax.rem(lax.axis_index("dp"), 2)

    def put(slot, ref):
        return pltpu.make_async_copy(acc.at[slot], ref, sem.at[slot])

    @pl.when(core == 0)
    def _():
        put(0, xg_ref).start()
        put(1, yg_ref).start()

    @pl.when(core == 1)
    def _():
        put(0, yg_ref).start()
        put(1, xg_ref).start()

    put(0, xg_ref).wait()
    put(1, yg_ref).wait()


def per_device(n, images, texts, log_scale, bias):
    rows, width = images.shape
    block = (rows, width)
    hbm = [pltpu.with_memory_space_constraint(z, pltpu.HBM) for z in (images, texts)]
    grads = pl.pallas_call(
        functools.partial(kernel, n),
        out_shape=pltpu.VMEM((2, *block), jnp.float32),
        in_specs=[pl.BlockSpec(memory_space=pl.ANY)] * 2 + [pl.BlockSpec(memory_space=pltpu.SMEM)] * 2,
        out_specs=pl.BlockSpec(memory_space=pltpu.VMEM),
        scratch_shapes=[
            pltpu.VMEM((8, *block), jnp.float32),
            pltpu.VMEM((2, *block), jnp.bfloat16),
            pltpu.VMEM((2, *block), jnp.bfloat16),
            pltpu.VMEM((3 * rows // 2, width), jnp.bfloat16),
            pltpu.VMEM((1, rows // 2), jnp.float32),
            pltpu.SemaphoreType.DMA((2,)),
            pltpu.SemaphoreType.DMA((8, 2)),
            pltpu.SemaphoreType.DMA((8, 2)),
            pltpu.SemaphoreType.REGULAR,
        ],
        compiler_params=pltpu.CompilerParams(collective_id=0, has_side_effects=True, vmem_limit_bytes=40 * 2**20),
    )(*hbm, log_scale, bias)
    return pl.pallas_call(
        place,
        out_shape=(pltpu.HBM(block, jnp.float32),) * 2,
        in_specs=[pl.BlockSpec(memory_space=pl.ANY)],
        out_specs=(pl.BlockSpec(memory_space=pl.ANY),) * 2,
        scratch_shapes=[pltpu.SemaphoreType.DMA((2,))],
    )(pltpu.with_memory_space_constraint(grads, pltpu.VMEM))


def solution(mesh):
    return jax.shard_map(
        functools.partial(per_device, mesh.shape["dp"]),
        mesh=mesh,
        in_specs=(P("dp", None), P("dp", None), P(), P()),
        out_specs=(P("dp", None), P("dp", None)),
        check_vma=False,
    )
```

```python
import functools

import jax
import jax.numpy as jnp
from jax import lax
from jax.experimental import pallas as pl
from jax.experimental.pallas import tpu as pltpu
from jax.sharding import PartitionSpec as P

MESH = pl.DeviceIdType.MESH
A, B, SIB, D1, D2, D3, E2, E3 = range(8)
NT = (((1,), (1,)), ((), ()))
START = ((B, 0), (B, 1), (A, 0), (A, 1), (SIB, 0), (SIB, 1))
LOCAL = len(START)
USUAL = START + ((E2, 0), (D2, 0), (D1, 0), (E3, 0), (E2, 1), (D2, 1), (D1, 1), (E3, 1), (D3, 0), (D3, 1))
FIRST = (
    START + ((E3, 0), (E2, 0), (D1, 0), (E3, 1), (E2, 1), (D1, 1), (D2, 0), (D2, 1), (D3, 0), (D3, 1)),
    START + ((D2, 0), (D1, 0), (E2, 0), (D2, 1), (E2, 1), (D1, 1), (E3, 0), (D3, 0), (E3, 1), (D3, 1)),
)
LAST = (
    START + ((E2, 0), (D2, 0), (D1, 0), (D2, 1), (D1, 1), (E3, 0), (E2, 1), (E3, 1), (D3, 0), (D3, 1)),
    START + ((E2, 0), (D1, 0), (E3, 0), (D2, 0), (E2, 1), (D1, 1), (E3, 1), (D2, 1), (D3, 0), (D3, 1)),
)


def halves(value):
    high = value.astype(jnp.bfloat16)
    return high, (value - high.astype(jnp.float32)).astype(jnp.bfloat16)


def dot(a, b, dims=(((1,), (0,)), ((), ()))):
    return lax.dot_general(a, b, dims, preferred_element_type=jnp.float32)


def pick(index, values):
    result = values[0]
    for k in range(1, len(values)):
        if values[k] != values[k - 1]:
            result = jnp.where(index >= k, values[k], result)
    return result


def kernel(n, x_ref, y_ref, ls_ref, bias_ref, acc, pool, high, low, stack, scale, load_sem, send_sem, recv_sem, left_sem):
    me = lax.axis_index("dp")
    core, chip = lax.rem(me, 2), lax.div(me, 2)
    sib = me + 1 - 2 * core
    right, left = lax.rem(me + 2, n), lax.rem(me + n - 2, n)
    front, back = lax.rem(me + n - 2 + 4 * core, n), lax.rem(me + n + 2 - 4 * core, n)
    rows = pool.shape[1]
    half = rows // 2
    first, last = chip == 0, chip == n // 2 - 1

    barrier = pltpu.get_barrier_semaphore()

    def greet(peer):
        pl.semaphore_signal(barrier, inc=1, device_id=(peer,), device_id_type=MESH)

    cross = lax.rem(me + n - 1 + 2 * core, n)
    opens, early, closes = first & (core == 0), first & (core == 1), last & (core == 1)
    greet(sib)
    greet(left)
    pl.when(jnp.logical_not(last))(lambda: greet(right))
    pl.when(jnp.logical_not(closes))(lambda: greet(cross))

    def load(slot, ref):
        return pltpu.make_async_copy(ref, pool.at[slot], load_sem.at[slot])

    @pl.when(core == 0)
    def _():
        load(A, x_ref).start()
        load(B, y_ref).start()

    @pl.when(core == 1)
    def _():
        load(A, y_ref).start()
        load(B, x_ref).start()

    def transfer(src, dst, sent, received, peer):
        return pltpu.make_async_remote_copy(
            src_ref=src, dst_ref=dst, send_sem=sent, recv_sem=received, device_id=(peer,), device_id_type=MESH
        )

    def copy(src, dst, at, sent, received, peer):
        return transfer(pool.at[src, at], pool.at[dst, at], sent, received, peer)

    def send(src, dst, h, peer):
        return copy(src, dst, pl.ds(h * half, half), send_sem.at[dst, h], recv_sem.at[dst, h], peer)

    def relay(src, h, piece, sent, peer):
        at = pl.ds(h * half + piece * (half // 2), half // 2)
        return copy(src, D3, at, send_sem.at[sent, h], recv_sem.at[(D3, A)[piece], h], peer)

    def send_a(h):
        return send(A, E2, h, front)

    def send_b(h):
        return send(B, D2, h, back)

    def send_sib(h):
        return send(B, SIB, h, sib)

    def pass_e2(h):
        return send(E2, D1, h, sib)

    def pass_d2(h):
        return send(D2, E3, h, sib)

    def relay_d1(h):
        return relay(D1, h, 0, D3, back)

    def relay_e2(h):
        return relay(E2, h, 1, A, cross)

    def stand_in(h):
        return relay(E2, h, 0, B, cross)

    def start(which):
        which(0).start()
        which(1).start()

    pl.semaphore_wait(barrier, jnp.where(opens, 2, jnp.where(early, 3, 4)))
    pl.when(last)(lambda: pl.semaphore_signal(left_sem, inc=1, device_id=(right,), device_id_type=MESH))
    pl.when(closes)(lambda: pl.semaphore_signal(left_sem, inc=1, device_id=(cross,), device_id_type=MESH))
    behind = early | (last & (core == 0))

    def start_from(ref, dst, peer):
        for h in range(2):
            at = pl.ds(h * half, half)
            transfer(ref.at[at], pool.at[dst, at], send_sem.at[dst, h], recv_sem.at[dst, h], peer).start()

    for parity, (a_ref, b_ref) in enumerate(((x_ref, y_ref), (y_ref, x_ref))):
        here = core == parity
        pl.when(here & jnp.logical_not(opens))(functools.partial(start_from, a_ref, E2, front))
        pl.when(here & jnp.logical_not(behind))(functools.partial(start_from, b_ref, D2, back))
        pl.when(here)(functools.partial(start_from, b_ref, SIB, sib))
    acc[...] = jnp.zeros_like(acc)
    scale[...] = jnp.exp(jnp.full(scale.shape, ls_ref[0], jnp.float32))
    offset = bias_ref[0]
    load(A, x_ref).wait()
    load(B, y_ref).wait()
    for slot in range(2):
        high[slot], low[slot] = halves(pool[slot])

    def take_e2(h):
        send_a(h).wait_recv()
        pass_e2(h).start()
        waits = opens | closes
        pl.when(jnp.logical_not(waits))(lambda: relay_e2(h).start())
        if h == 1:
            pl.when(waits)(lambda: start(relay_e2))
            pl.when(opens)(lambda: start(stand_in))

    def take_d2(h):
        send_b(h).wait_recv()
        pass_d2(h).start()

    def take_d1(h):
        pass_e2(h).wait_recv()
        pl.when(jnp.logical_not(early))(lambda: relay_d1(h).start())

    def open_left():
        pl.when(early)(lambda: pl.semaphore_wait(left_sem, 1))
        pl.when(opens)(lambda: pl.semaphore_wait(left_sem, 2))
        pl.when(opens)(lambda: start(send_a))

    def start_later():
        pl.when(behind)(lambda: start(send_b))

    def add_pairs(mine, slot, h):
        at = pl.multiple_of(h * half, half)
        oh, ol = halves(pool[slot, pl.ds(at, half)])
        stack[:half], stack[half : 2 * half], stack[2 * half :] = oh, ol, oh
        times = scale[...]
        wide = dot(high[mine], stack[: 2 * half], NT)
        logits = (wide[:, :half] + (wide[:, half:] + dot(low[mine], oh, NT))) * times + offset
        shape = (rows, half)
        gap = lax.broadcasted_iota(jnp.int32, shape, 0) - lax.broadcasted_iota(jnp.int32, shape, 1)
        positive = gap == jnp.where(slot <= B, at, rows)
        grads = jnp.where(positive, -times, times) / (1.0 + jnp.exp(jnp.where(positive, logits, -logits)))
        gh, gl = halves(grads)
        acc[mine] += dot(jnp.concatenate([gh, gh, gl], axis=1), stack[...])

    def by_place(usual, zero, one, last_zero, last_one):
        ends = jnp.where(first, jnp.where(core == 0, zero, one), jnp.where(core == 0, last_zero, last_one))
        return jnp.where(first | last, ends, usual)

    def step_of(block, h):
        return by_place(*(tasks.index((block, h)) for tasks in (USUAL, *FIRST, *LAST)))

    def recv(which, h):
        return lambda: which(h).wait_recv()

    events = [(jnp.int32(LOCAL), open_left), (jnp.int32(LOCAL), start_later)]
    for h in range(2):
        events += [
            (step_of(SIB, h), recv(send_sib, h)),
            (step_of(E2, h), functools.partial(take_e2, h)),
            (step_of(D2, h), functools.partial(take_d2, h)),
            (step_of(E3, h), recv(pass_d2, h)),
            (step_of(D1, h), functools.partial(take_d1, h)),
            (step_of(D3, h), recv(relay_d1, h)),
            (step_of(D3, h), recv(relay_e2, h)),
        ]

    def by_order(i, part):
        return [pick(i, [task[part] for task in tasks]) for tasks in (USUAL, *FIRST, *LAST)]

    def step(i, _):
        for at_step, event in events:
            pl.when(i == at_step)(event)
        slot, h = (by_place(*by_order(i, part)) for part in range(2))
        mine = jnp.where((slot == A) | (slot == SIB) | (slot >= E2), 1, 0)
        add_pairs(mine, slot, h)
        return 0

    lax.fori_loop(0, len(USUAL), step, 0)

    for h in range(2):
        for which in (send_a, send_b, send_sib, pass_e2, pass_d2):
            which(h).wait_send()
        relay_e2(h).wait_send()
        pl.when(jnp.logical_not(early))(lambda: relay_d1(h).wait_send())
        pl.when(opens)(lambda: stand_in(h).wait_send())


def place(acc, xg_ref, yg_ref, sem):
    core = lax.rem(lax.axis_index("dp"), 2)

    def put(slot, ref):
        return pltpu.make_async_copy(acc.at[slot], ref, sem.at[slot])

    @pl.when(core == 0)
    def _():
        put(0, xg_ref).start()
        put(1, yg_ref).start()

    @pl.when(core == 1)
    def _():
        put(0, yg_ref).start()
        put(1, xg_ref).start()

    put(0, xg_ref).wait()
    put(1, yg_ref).wait()


def per_device(n, images, texts, log_scale, bias):
    rows, width = images.shape
    block = (rows, width)
    hbm = [pltpu.with_memory_space_constraint(z, pltpu.HBM) for z in (images, texts)]
    grads = pl.pallas_call(
        functools.partial(kernel, n),
        out_shape=pltpu.VMEM((2, *block), jnp.float32),
        in_specs=[pl.BlockSpec(memory_space=pl.ANY)] * 2 + [pl.BlockSpec(memory_space=pltpu.SMEM)] * 2,
        out_specs=pl.BlockSpec(memory_space=pltpu.VMEM),
        scratch_shapes=[
            pltpu.VMEM((8, *block), jnp.float32),
            pltpu.VMEM((2, *block), jnp.bfloat16),
            pltpu.VMEM((2, *block), jnp.bfloat16),
            pltpu.VMEM((3 * rows // 2, width), jnp.bfloat16),
            pltpu.VMEM((1, rows // 2), jnp.float32),
            pltpu.SemaphoreType.DMA((2,)),
            pltpu.SemaphoreType.DMA((8, 2)),
            pltpu.SemaphoreType.DMA((8, 2)),
            pltpu.SemaphoreType.REGULAR,
        ],
        compiler_params=pltpu.CompilerParams(collective_id=0, has_side_effects=True, vmem_limit_bytes=40 * 2**20),
    )(*hbm, log_scale, bias)
    return pl.pallas_call(
        place,
        out_shape=(pltpu.HBM(block, jnp.float32),) * 2,
        in_specs=[pl.BlockSpec(memory_space=pl.ANY)],
        out_specs=(pl.BlockSpec(memory_space=pl.ANY),) * 2,
        scratch_shapes=[pltpu.SemaphoreType.DMA((2,))],
    )(pltpu.with_memory_space_constraint(grads, pltpu.VMEM))


def solution(mesh):
    return jax.shard_map(
        functools.partial(per_device, mesh.shape["dp"]),
        mesh=mesh,
        in_specs=(P("dp", None), P("dp", None), P(), P()),
        out_specs=(P("dp", None), P("dp", None)),
        check_vma=False,
    )
```

```python
import functools

import jax
import jax.numpy as jnp
from jax import lax
from jax.experimental import pallas as pl
from jax.experimental.pallas import tpu as pltpu
from jax.sharding import PartitionSpec as P

MESH = pl.DeviceIdType.MESH
A, B, SIB, D1, D2, D3, E2, E3 = range(8)
NT = (((1,), (1,)), ((), ()))
START = ((B, 0), (B, 1), (A, 0), (A, 1), (SIB, 0), (SIB, 1))
LOCAL = len(START)
USUAL = START + ((E2, 0), (D2, 0), (D1, 0), (E3, 0), (E2, 1), (D2, 1), (D1, 1), (E3, 1), (D3, 0), (D3, 1))
FIRST = (
    START + ((E3, 0), (E2, 0), (D1, 0), (E3, 1), (E2, 1), (D1, 1), (D2, 0), (D2, 1), (D3, 0), (D3, 1)),
    START + ((D2, 0), (D1, 0), (E2, 0), (D2, 1), (E2, 1), (D1, 1), (E3, 0), (D3, 0), (E3, 1), (D3, 1)),
)
LAST = (
    START + ((E2, 0), (D2, 0), (D1, 0), (D2, 1), (D1, 1), (E3, 0), (E2, 1), (E3, 1), (D3, 0), (D3, 1)),
    START + ((E2, 0), (D1, 0), (E3, 0), (E2, 1), (D2, 0), (D1, 1), (E3, 1), (D2, 1), (D3, 0), (D3, 1)),
)


def halves(value):
    high = value.astype(jnp.bfloat16)
    return high, (value - high.astype(jnp.float32)).astype(jnp.bfloat16)


def dot(a, b, dims=(((1,), (0,)), ((), ()))):
    return lax.dot_general(a, b, dims, preferred_element_type=jnp.float32)


def pick(index, values):
    result = values[0]
    for k in range(1, len(values)):
        if values[k] != values[k - 1]:
            result = jnp.where(index >= k, values[k], result)
    return result


def kernel(n, x_ref, y_ref, ls_ref, bias_ref, acc, pool, high, low, stack, scale, load_sem, send_sem, recv_sem, left_sem):
    me = lax.axis_index("dp")
    core, chip = lax.rem(me, 2), lax.div(me, 2)
    sib = me + 1 - 2 * core
    right, left = lax.rem(me + 2, n), lax.rem(me + n - 2, n)
    front, back = lax.rem(me + n - 2 + 4 * core, n), lax.rem(me + n + 2 - 4 * core, n)
    rows = pool.shape[1]
    half = rows // 2
    first, last = chip == 0, chip == n // 2 - 1

    barrier = pltpu.get_barrier_semaphore()

    def greet(peer):
        pl.semaphore_signal(barrier, inc=1, device_id=(peer,), device_id_type=MESH)

    cross = lax.rem(me + n - 1 + 2 * core, n)
    opens, early, closes = first & (core == 0), first & (core == 1), last & (core == 1)
    greet(sib)
    greet(left)
    near, ends = chip == n // 2 - 2, last & (core == 0)
    pl.when(jnp.logical_not(last | near))(lambda: greet(right))
    pl.when(jnp.logical_not(closes | (near & (core == 1))))(lambda: greet(cross))

    def load(slot, ref):
        return pltpu.make_async_copy(ref, pool.at[slot], load_sem.at[slot])

    @pl.when(core == 0)
    def _():
        load(A, x_ref).start()
        load(B, y_ref).start()

    @pl.when(core == 1)
    def _():
        load(A, y_ref).start()
        load(B, x_ref).start()

    def transfer(src, dst, sent, received, peer):
        return pltpu.make_async_remote_copy(
            src_ref=src, dst_ref=dst, send_sem=sent, recv_sem=received, device_id=(peer,), device_id_type=MESH
        )

    def copy(src, dst, at, sent, received, peer):
        return transfer(pool.at[src, at], pool.at[dst, at], sent, received, peer)

    def send(src, dst, h, peer):
        return copy(src, dst, pl.ds(h * half, half), send_sem.at[dst, h], recv_sem.at[dst, h], peer)

    def relay(src, h, piece, sent, peer):
        at = pl.ds(h * half + piece * (half // 2), half // 2)
        return copy(src, D3, at, send_sem.at[sent, h], recv_sem.at[(D3, A)[piece], h], peer)

    def send_a(h):
        return send(A, E2, h, front)

    def send_b(h):
        return send(B, D2, h, back)

    def send_sib(h):
        return send(B, SIB, h, sib)

    def pass_e2(h):
        return send(E2, D1, h, sib)

    def pass_d2(h):
        return send(D2, E3, h, sib)

    def relay_d1(h):
        return relay(D1, h, 0, D3, back)

    def relay_e2(h):
        return relay(E2, h, 1, A, cross)

    def stand_in(h):
        return relay(E2, h, 0, B, cross)

    def start(which):
        which(0).start()
        which(1).start()

    pl.semaphore_wait(barrier, jnp.where(opens | ends, 2, jnp.where(early | closes, 3, 4)))
    pl.when(last | near)(lambda: pl.semaphore_signal(left_sem, inc=1, device_id=(right,), device_id_type=MESH))
    pl.when(closes | (near & (core == 1)))(lambda: pl.semaphore_signal(left_sem, inc=1, device_id=(cross,), device_id_type=MESH))
    behind = early | ends

    def start_from(ref, dst, peer):
        for h in range(2):
            at = pl.ds(h * half, half)
            transfer(ref.at[at], pool.at[dst, at], send_sem.at[dst, h], recv_sem.at[dst, h], peer).start()

    for parity, (a_ref, b_ref) in enumerate(((x_ref, y_ref), (y_ref, x_ref))):
        here = core == parity
        pl.when(here & jnp.logical_not(opens | ends))(functools.partial(start_from, a_ref, E2, front))
        pl.when(here & jnp.logical_not(behind | closes))(functools.partial(start_from, b_ref, D2, back))
        pl.when(here)(functools.partial(start_from, b_ref, SIB, sib))

    @pl.when(ends)
    def _():
        pl.semaphore_wait(left_sem, 2)
        start_from(x_ref, E2, front)

    @pl.when(closes)
    def _():
        pl.semaphore_wait(left_sem, 1)
        start_from(x_ref, D2, back)

    acc[...] = jnp.zeros_like(acc)
    scale[...] = jnp.exp(jnp.full(scale.shape, ls_ref[0], jnp.float32))
    offset = bias_ref[0]
    load(A, x_ref).wait()
    load(B, y_ref).wait()
    for slot in range(2):
        high[slot], low[slot] = halves(pool[slot])

    def take_e2(h):
        send_a(h).wait_recv()
        pass_e2(h).start()
        waits = opens | closes
        pl.when(jnp.logical_not(waits))(lambda: relay_e2(h).start())
        if h == 1:
            pl.when(waits)(lambda: start(relay_e2))
            pl.when(opens)(lambda: start(stand_in))

    def take_d2(h):
        send_b(h).wait_recv()
        pass_d2(h).start()

    def take_d1(h):
        pass_e2(h).wait_recv()
        pl.when(jnp.logical_not(early))(lambda: relay_d1(h).start())

    def open_left():
        pl.when(early)(lambda: pl.semaphore_wait(left_sem, 1))
        pl.when(opens)(lambda: pl.semaphore_wait(left_sem, 2))
        pl.when(opens)(lambda: start(send_a))

    def start_later():
        pl.when(behind)(lambda: start(send_b))

    def add_pairs(mine, slot, h):
        at = pl.multiple_of(h * half, half)
        oh, ol = halves(pool[slot, pl.ds(at, half)])
        stack[:half], stack[half : 2 * half], stack[2 * half :] = oh, ol, oh
        times = scale[...]
        wide = dot(high[mine], stack[: 2 * half], NT)
        logits = (wide[:, :half] + (wide[:, half:] + dot(low[mine], oh, NT))) * times + offset
        shape = (rows, half)
        gap = lax.broadcasted_iota(jnp.int32, shape, 0) - lax.broadcasted_iota(jnp.int32, shape, 1)
        positive = gap == jnp.where(slot <= B, at, rows)
        grads = jnp.where(positive, -times, times) / (1.0 + jnp.exp(jnp.where(positive, logits, -logits)))
        gh, gl = halves(grads)
        acc[mine] += dot(jnp.concatenate([gh, gh, gl], axis=1), stack[...])

    def by_place(usual, zero, one, last_zero, last_one):
        ends = jnp.where(first, jnp.where(core == 0, zero, one), jnp.where(core == 0, last_zero, last_one))
        return jnp.where(first | last, ends, usual)

    def step_of(block, h):
        return by_place(*(tasks.index((block, h)) for tasks in (USUAL, *FIRST, *LAST)))

    def recv(which, h):
        return lambda: which(h).wait_recv()

    events = [(jnp.int32(LOCAL), open_left), (jnp.int32(LOCAL), start_later)]
    for h in range(2):
        events += [
            (step_of(SIB, h), recv(send_sib, h)),
            (step_of(E2, h), functools.partial(take_e2, h)),
            (step_of(D2, h), functools.partial(take_d2, h)),
            (step_of(E3, h), recv(pass_d2, h)),
            (step_of(D1, h), functools.partial(take_d1, h)),
            (step_of(D3, h), recv(relay_d1, h)),
            (step_of(D3, h), recv(relay_e2, h)),
        ]

    def by_order(i, part):
        return [pick(i, [task[part] for task in tasks]) for tasks in (USUAL, *FIRST, *LAST)]

    def step(i, _):
        for at_step, event in events:
            pl.when(i == at_step)(event)
        slot, h = (by_place(*by_order(i, part)) for part in range(2))
        mine = jnp.where((slot == A) | (slot == SIB) | (slot >= E2), 1, 0)
        add_pairs(mine, slot, h)
        return 0

    lax.fori_loop(0, len(USUAL), step, 0)

    for h in range(2):
        for which in (send_a, send_b, send_sib, pass_e2, pass_d2):
            which(h).wait_send()
        relay_e2(h).wait_send()
        pl.when(jnp.logical_not(early))(lambda: relay_d1(h).wait_send())
        pl.when(opens)(lambda: stand_in(h).wait_send())


def place(acc, xg_ref, yg_ref, sem):
    core = lax.rem(lax.axis_index("dp"), 2)

    def put(slot, ref):
        return pltpu.make_async_copy(acc.at[slot], ref, sem.at[slot])

    @pl.when(core == 0)
    def _():
        put(0, xg_ref).start()
        put(1, yg_ref).start()

    @pl.when(core == 1)
    def _():
        put(0, yg_ref).start()
        put(1, xg_ref).start()

    put(0, xg_ref).wait()
    put(1, yg_ref).wait()


def per_device(n, images, texts, log_scale, bias):
    rows, width = images.shape
    block = (rows, width)
    hbm = [pltpu.with_memory_space_constraint(z, pltpu.HBM) for z in (images, texts)]
    grads = pl.pallas_call(
        functools.partial(kernel, n),
        out_shape=pltpu.VMEM((2, *block), jnp.float32),
        in_specs=[pl.BlockSpec(memory_space=pl.ANY)] * 2 + [pl.BlockSpec(memory_space=pltpu.SMEM)] * 2,
        out_specs=pl.BlockSpec(memory_space=pltpu.VMEM),
        scratch_shapes=[
            pltpu.VMEM((8, *block), jnp.float32),
            pltpu.VMEM((2, *block), jnp.bfloat16),
            pltpu.VMEM((2, *block), jnp.bfloat16),
            pltpu.VMEM((3 * rows // 2, width), jnp.bfloat16),
            pltpu.VMEM((1, rows // 2), jnp.float32),
            pltpu.SemaphoreType.DMA((2,)),
            pltpu.SemaphoreType.DMA((8, 2)),
            pltpu.SemaphoreType.DMA((8, 2)),
            pltpu.SemaphoreType.REGULAR,
        ],
        compiler_params=pltpu.CompilerParams(collective_id=0, has_side_effects=True, vmem_limit_bytes=40 * 2**20),
    )(*hbm, log_scale, bias)
    return pl.pallas_call(
        place,
        out_shape=(pltpu.HBM(block, jnp.float32),) * 2,
        in_specs=[pl.BlockSpec(memory_space=pl.ANY)],
        out_specs=(pl.BlockSpec(memory_space=pl.ANY),) * 2,
        scratch_shapes=[pltpu.SemaphoreType.DMA((2,))],
    )(pltpu.with_memory_space_constraint(grads, pltpu.VMEM))


def solution(mesh):
    return jax.shard_map(
        functools.partial(per_device, mesh.shape["dp"]),
        mesh=mesh,
        in_specs=(P("dp", None), P("dp", None), P(), P()),
        out_specs=(P("dp", None), P("dp", None)),
        check_vma=False,
    )
```
